512 devices in a mesh: row: 8 (over y), col: 32 (over z, x), layer: 2 (over core).
Axes of the slice: x: 4, y: 8, z: 8, core: 2. Of those that a mesh axis runs over, the one named last changes fastest.
Arguments:
- s_values: bfloat16 [8, 32, 2, 128, 128], P('row', 'col'), may hold values from -0.5 to 0.5
- s_slots: int32 [8, 32, 2], P('row', 'col'), may hold values from 0 to 16, as said below
- x_values: bfloat16 [4, 8, 32, 1, 128, 128], P(None, 'row', 'col'), may hold values from -6 to 6
- x_slots: int32 [4, 8, 32, 1], P(None, 'row', 'col'), may hold values from 0 to 3, as said below
Outputs:
- product: float32 [8192, 8192], P(('row', 'layer'), 'col')
The draws below stay inside these ranges and needn't reach their ends.
Inputs may be any that keep to these rules, and one draw needn't show every extreme that they name: `s_slots`: within one piece the live values are distinct; the value 8 * 2 marks an empty slot, empty slots follow the live ones, every piece has at least one live slot, and at least one piece has all 2 slots live. `x_slots`: within one piece the 1 positions are distinct.
All inputs are finite; a program needn't handle non-finite values.
Results may differ from the reference program's by a relative error of at most 0.0003.
Values may be sent and summed in bfloat16 or wider, within the bound.
A program may use at most 64 MiB of HBM per device.

```python
import jax
import jax.numpy as jnp

B = 128
BR = 8
BC = 2
BK = 2
KS = 2
KX = 1
Q = 4
NB = 64
NCB = 64
N_ROW = 8
N_COL = 32


def draw_s_slots(key, part):
    key = jax.random.fold_in(key, 11)
    region = BR * BK
    pieces = N_ROW * N_COL
    keys = jax.random.split(key, pieces + 2)
    orders = jax.vmap(lambda one_key: jax.random.permutation(one_key, region))(keys[:pieces])[:, :KS]
    counts = jax.random.randint(keys[pieces], (pieces,), max(1, KS // 4), KS + 1)
    fullest = jax.random.randint(keys[pieces + 1], (), 0, pieces)
    counts = jnp.where(jnp.arange(pieces) == fullest, KS, counts)
    slots = jnp.where(jnp.arange(KS)[None, :] < counts[:, None], orders, region)
    return slots.reshape(N_ROW, N_COL, KS).astype(jnp.int32)


def draw_x_slots(key, part):
    key = jax.random.fold_in(key, 23)
    region = BK * BC
    pieces = Q * N_ROW * N_COL
    keys = jax.random.split(key, pieces)
    orders = jax.vmap(lambda one_key: jax.random.permutation(one_key, region))(keys)[:, :KX]
    return orders.reshape(Q, N_ROW, N_COL, KX).astype(jnp.int32)


def levels(key, extent, cuts, least, high):
    gain = 1.0
    for axis_at, blocks in cuts:
        heights = jax.random.uniform(jax.random.fold_in(jax.random.fold_in(key, 6), axis_at), (blocks,), jnp.float32, least / len(cuts), high / len(cuts))
        gain = gain * jnp.repeat(jnp.exp(heights), extent[axis_at] // blocks).reshape((-1,) + (1,) * (len(extent) - 1 - axis_at))
    return gain


def gaussian(stream_key, extent, spread, limit, cuts=(), kind=jnp.bfloat16):
    factor_of = levels(stream_key, extent, cuts, -0.22, 0.18) if cuts else 1.0
    result = jax.random.normal(stream_key, extent, jnp.float32) * spread * factor_of
    return jnp.minimum(jnp.maximum(result, -limit), limit).astype(kind)


def setup_inputs(seed: int = 0) -> dict:
    splits = jax.random.split(jax.random.key(seed), 5)
    return {
        "s_values": gaussian(splits[0], (N_ROW, N_COL, KS, B, B), B ** -0.5, 0.5, ((0, 8), (1, 32))),
        "s_slots": draw_s_slots(jax.random.fold_in(splits[4], 71), 0),
        "x_values": gaussian(splits[2], (Q, N_ROW, N_COL, KX, B, B), 1.0, 6.0, ((1, 8), (2, 32))),
        "x_slots": draw_x_slots(jax.random.fold_in(splits[4], 71), 0),
    }


def reference(s_values, s_slots, x_values, x_slots):
    region = BR * BK
    live = s_slots < region
    safe_slots = jnp.where(live, s_slots, 0)
    row_group = jnp.arange(N_ROW, dtype=jnp.int32)[:, None, None]
    piece_index = jnp.arange(N_COL, dtype=jnp.int32)[None, :, None]
    block_rows = row_group * BR + safe_slots // BK
    block_cols = piece_index * BK + safe_slots % BK
    kept = jnp.where(live[..., None, None], s_values.astype(jnp.float32), jnp.float32(0.0))
    s_blocks = jnp.zeros((NB, NB, B, B), jnp.float32).at[block_rows, block_cols].add(kept)
    margin = s_blocks.transpose(0, 2, 1, 3).reshape(NB * B, NB * B).astype(jnp.bfloat16)
    group_index = jnp.arange(Q, dtype=jnp.int32)[:, None, None, None]
    residue = jnp.arange(N_ROW, dtype=jnp.int32)[None, :, None, None]
    column_group = jnp.arange(N_COL, dtype=jnp.int32)[None, None, :, None]
    x_rows = (group_index * N_ROW + residue) * BK + x_slots // BC
    x_cols = column_group * BC + x_slots % BC
    x_blocks = jnp.zeros((NB, NCB, B, B), jnp.float32).at[x_rows, x_cols].add(x_values.astype(jnp.float32))
    density = x_blocks.transpose(0, 2, 1, 3).reshape(NB * B, NCB * B).astype(jnp.bfloat16)
    return jnp.dot(margin, density, preferred_element_type=jnp.float32)
```

```python
import jax
import jax.numpy as jnp
from jax import lax
from jax.experimental import pallas as pl
from jax.experimental.pallas import tpu as pltpu
from jax.sharding import PartitionSpec as P

MESH = pl.DeviceIdType.MESH
NY, NZ, NX, NL = 8, 8, 4, 2
B = 128

S_PATH = {
    (1, 0): (0, 0), (7, 0): (0, 0), (2, 0): (0, 0), (6, 0): (0, 0),
    (3, 0): (0, 0), (5, 0): (0, 0), (4, 0): (0, 0),
}
for _z in (0, 1, 7, 2, 6, 3, 5, 4):
    S_PATH[_z, 1] = (_z, 0)
    S_PATH[_z, 3] = (_z, 0)
for _z in (0, 1, 7, 2, 6, 3, 5, 4):
    S_PATH[_z, 2] = (_z, 1 if _z % 2 else 3)
S_ORDER = list(S_PATH)
X_PATH = {1: 0, 7: 0, 2: 0, 6: 0, 3: 2, 5: 6, 4: 2}
X_ORDER = [1, 7, 2, 6, 3, 5, 4]
EVENTS = None


def steps():
    s_steps = {(b[0] - a[0], b[1] - a[1]) for b, a in S_PATH.items()}
    x_steps = {b - a for b, a in X_PATH.items()}
    found = {(0, dz % NZ, dx % NX) for dz, dx in s_steps}
    found |= {(0, -dz % NZ, -dx % NX) for dz, dx in s_steps}
    found |= {(dy % NY, 0, 0) for dy in x_steps} | {(-dy % NY, 0, 0) for dy in x_steps}
    return sorted(found)


def kernel(s_hbm, ss_hbm, x_hbm, xs_hbm, out, sbuf, xbuf, sl, xl, dummy, ssm, xsm,
           s_sem, x_sem, sib_s, sib_x, send, local):
    y = lax.axis_index("row")
    col = lax.axis_index("col")
    l = lax.axis_index("layer")
    z, x = col // NX, col % NX
    sg = 1 - 2 * l

    def place(dy, dz, dx):
        return (
            lax.rem(y + sg * dy + NY, NY),
            lax.rem(z + sg * dz + NZ, NZ) * NX + lax.rem(x + sg * dx + NX, NX),
            l,
        )

    sibling = (y, col, 1 - l)
    peers = steps()
    barrier = pltpu.get_barrier_semaphore()
    for peer in peers:
        pl.semaphore_signal(barrier, inc=1, device_id=place(*peer), device_id_type=MESH)
    pl.semaphore_signal(barrier, inc=1, device_id=sibling, device_id_type=MESH)

    loads = [
        pltpu.make_async_copy(ss_hbm, ssm, local.at[0]),
        pltpu.make_async_copy(xs_hbm, xsm, local.at[1]),
        pltpu.make_async_copy(s_hbm.at[0, 0], sbuf.at[pl.ds(col * 2, 2)], local.at[2]),
        pltpu.make_async_copy(x_hbm.at[:, 0, 0, 0], xbuf.at[pl.ds(y * 4, 4)], local.at[3]),
    ]
    for load in loads:
        load.start()
    loads[0].wait()
    loads[1].wait()
    for a in range(2):
        sl[col * 2 + a] = jnp.full((1, B), ssm[0, 0, a], jnp.int32)
    for m in range(4):
        xl[y * 4 + m] = jnp.full((1, B), xsm[m, 0, 0, 0], jnp.int32)
    loads[2].wait()
    loads[3].wait()
    pl.semaphore_wait(barrier, len(peers) + 1)

    s_index = {o: i for i, o in enumerate(S_ORDER)}
    x_index = {o: i for i, o in enumerate(X_ORDER)}

    def s_origin(o):
        return lax.rem(z - sg * o[0] + NZ, NZ) * NX + lax.rem(x - sg * o[1] + NX, NX)

    def x_origin(o):
        return lax.rem(y - sg * o + NY, NY)

    def wait_bytes(ref, sem):
        pltpu.make_async_copy(ref, ref, sem).wait()

    def send_s(o):
        piece = s_origin(o)
        block = sbuf.at[pl.ds(piece * 2 + l, 1)]
        slots = sl.at[pl.ds(piece * 2, 2)]
        for child, parent in S_PATH.items():
            if parent == o:
                to = place(0, (child[0] - o[0]) % NZ, (child[1] - o[1]) % NX)
                got = s_sem.at[s_index[child]]
                pltpu.make_async_remote_copy(block, block, send.at[0], got, device_id=to, device_id_type=MESH).start()
                pltpu.make_async_remote_copy(slots, slots, send.at[1], got, device_id=to, device_id_type=MESH).start()
        if o != (0, 0):
            pltpu.make_async_remote_copy(
                block, block, send.at[2], sib_s.at[o[0] % NZ], device_id=sibling, device_id_type=MESH
            ).start()

    def send_x(o):
        origin = x_origin(o)
        block = xbuf.at[pl.ds(origin * 4 + l * 2, 2)]
        slots = xl.at[pl.ds(origin * 4, 4)]
        for child, parent in X_PATH.items():
            if parent == o:
                to = place((child - o) % NY, 0, 0)
                got = x_sem.at[x_index[child]]
                pltpu.make_async_remote_copy(block, block, send.at[3], got, device_id=to, device_id_type=MESH).start()
                pltpu.make_async_remote_copy(slots, slots, send.at[4], got, device_id=to, device_id_type=MESH).start()
        if o != 0:
            pltpu.make_async_remote_copy(
                block, block, send.at[5], sib_x, device_id=sibling, device_id_type=MESH
            ).start()

    send_s((0, 0))
    send_x(0)
    events = EVENTS
    if events is None:
        events = [("x", o) for o in X_ORDER[:4]] + [("s", o) for o in S_ORDER[:12]]
        events += [("x", o) for o in X_ORDER[4:]] + [("s", o) for o in S_ORDER[12:]]
    for kind, o in events:
        if kind == "s":
            wait_bytes(dummy.at[pl.ds(0, 66)], s_sem.at[s_index[o]])
            send_s(o)
        else:
            wait_bytes(dummy, x_sem.at[x_index[o]])
            send_x(o)
    wait_bytes(xbuf.at[pl.ds(0, 14)], sib_x)

    def group(g, first):
        zz = lax.rem(z + sg * g + NZ, NZ)
        m, base = zz // 2, lax.rem(zz, 2) * 4
        x_tiles, masks, blocks = [], [], []
        for c in range(NX):
            xv = xbuf[(base + c) * 4 + m]
            xs = xl[(base + c) * 4 + m]
            odd = xs & 1
            put = jnp.broadcast_to(odd.astype(jnp.float32), (16, B)).astype(jnp.bfloat16)[None]
            keep = jnp.broadcast_to((1 - odd).astype(jnp.float32), (16, B)).astype(jnp.bfloat16)[None]
            parts = xv.reshape(8, 16, B)
            x_tiles.append(jnp.concatenate([(parts * keep).reshape(B, B), (parts * put).reshape(B, B)], axis=1))
            first_row = l * 8 + (xs >> 1)
            masks.append([sl[(zz * NX + c) * 2 + a] - first_row for a in range(2)])
            blocks.append([sbuf[(zz * NX + c) * 2 + a].reshape(8, 16, B) for a in range(2)])
        x_tile = jnp.concatenate(x_tiles, axis=0)
        for br in range(4):
            row = []
            for c in range(NX):
                hit = [
                    jnp.broadcast_to((masks[c][a] == 2 * br).astype(jnp.float32), (16, B)).astype(jnp.bfloat16)[None]
                    for a in range(2)
                ]
                row.append((blocks[c][0] * hit[0] + blocks[c][1] * hit[1]).reshape(B, B))
            part = jnp.dot(jnp.concatenate(row, axis=1), x_tile, preferred_element_type=jnp.float32)
            if first:
                out[pl.ds(br * B, B), :] = part
            else:
                out[pl.ds(br * B, B), :] += part

    for i, g in enumerate((0, 1, 7, 2, 6, 3, 5, 4)):
        wait_bytes(sbuf.at[pl.ds(0, 3 if g == 0 else 4)], sib_s.at[g])
        group(g, i == 0)
    wait_bytes(sbuf.at[pl.ds(0, 31)], send.at[0])
    wait_bytes(sl.at[pl.ds(0, 62)], send.at[1])
    wait_bytes(sbuf.at[pl.ds(0, 31)], send.at[2])
    wait_bytes(xbuf.at[pl.ds(0, 14)], send.at[3])
    wait_bytes(xl.at[pl.ds(0, 28)], send.at[4])
    wait_bytes(xbuf.at[pl.ds(0, 14)], send.at[5])


def per_device(s_values, s_slots, x_values, x_slots):
    return pl.pallas_call(
        kernel,
        out_shape=jax.ShapeDtypeStruct((512, 256), jnp.float32),
        in_specs=[pl.BlockSpec(memory_space=pl.ANY)] * 4,
        out_specs=pl.BlockSpec(memory_space=pltpu.VMEM),
        scratch_shapes=[
            pltpu.VMEM((64, B, B), jnp.bfloat16),
            pltpu.VMEM((32, B, B), jnp.bfloat16),
            pltpu.VMEM((64, 1, B), jnp.int32),
            pltpu.VMEM((32, 1, B), jnp.int32),
            pltpu.VMEM((132, 1, B), jnp.int32),
            pltpu.SMEM((1, 1, 2), jnp.int32),
            pltpu.SMEM((4, 1, 1, 1), jnp.int32),
            pltpu.SemaphoreType.DMA((31,)),
            pltpu.SemaphoreType.DMA((7,)),
            pltpu.SemaphoreType.DMA((8,)),
            pltpu.SemaphoreType.DMA,
            pltpu.SemaphoreType.DMA((6,)),
            pltpu.SemaphoreType.DMA((4,)),
        ],
        compiler_params=pltpu.CompilerParams(
            collective_id=0, has_side_effects=True, vmem_limit_bytes=48 * 2**20
        ),
        cost_estimate=pl.CostEstimate(flops=2**30, bytes_accessed=2**20, transcendentals=0),
        name="block_product",
    )(s_values, s_slots, x_values, x_slots)


def solution(mesh):
    placed = (
        P("row", "col", None, None, None),
        P("row", "col", None),
        P(None, "row", "col", None, None, None),
        P(None, "row", "col", None),
    )
    return jax.shard_map(
        per_device,
        mesh=mesh,
        in_specs=placed,
        out_specs=P(("row", "layer"), "col"),
        check_vma=False,
    )
```

```python
import jax
import jax.numpy as jnp
from jax import lax
from jax.experimental import pallas as pl
from jax.experimental.pallas import tpu as pltpu
from jax.sharding import PartitionSpec as P

MESH = pl.DeviceIdType.MESH
NY, NZ, NX = 8, 8, 4
B = 128
Y_PATH = {1: 0, 7: 0, 2: 0, 6: 0, 3: 2, 5: 6, 4: 2}
Y_ORDER = [1, 7, 2, 6, 3, 5, 4]
Y_STEPS = (1, 7, 2, 6)


def kernel(s_hbm, ss_hbm, x_hbm, xs_hbm, out, sbuf, xbuf, sl, xl, dummy, ssm, xsm,
           z_sem, x_sem, y_sem, sib_s, sib_x, send, local, ready):
    y = lax.axis_index("row")
    col = lax.axis_index("col")
    l = lax.axis_index("layer")
    z, x = col // NX, col % NX
    sg = 1 - 2 * l

    def on_z(to):
        return (y, to * NX + x, l)

    def on_x(step):
        return (y, z * NX + lax.rem(x + step, NX), l)

    def on_y(step):
        return (lax.rem(y + sg * step + NY, NY), col, l)

    sibling = (y, col, 1 - l)

    barrier = pltpu.get_barrier_semaphore()
    greeted = [sibling] + [on_x(s) for s in (1, 2, 3)] + [on_y(s) for s in Y_STEPS]
    for peer in greeted:
        pl.semaphore_signal(barrier, inc=1, device_id=peer, device_id_type=MESH)
    for to in range(1, NZ):
        @pl.when(z < to)
        def _():
            pl.semaphore_signal(barrier, inc=1, device_id=on_z(to), device_id_type=MESH)

    own = (l * NZ + z) * NX + x
    loads = [
        pltpu.make_async_copy(ss_hbm, ssm, local.at[0]),
        pltpu.make_async_copy(xs_hbm, xsm, local.at[1]),
        pltpu.make_async_copy(s_hbm.at[0, 0, pl.ds(l, 1)], sbuf.at[pl.ds(own, 1)], local.at[2]),
        pltpu.make_async_copy(
            x_hbm.at[pl.ds(l * 2, 2), 0, 0, 0], xbuf.at[pl.ds((l * NY + y) * 2, 2)], local.at[3]
        ),
    ]
    for load in loads:
        load.start()
    loads[0].wait()
    loads[1].wait()
    for a in range(2):
        sl[col * 2 + a] = jnp.full((1, B), ssm[0, 0, a], jnp.int32)
    for m in range(4):
        xl[y * 4 + m] = jnp.full((1, B), xsm[0, 0, 0, m], jnp.int32)
    pl.semaphore_wait(barrier, len(greeted) + z)
    for to in range(NZ - 1):
        @pl.when(z > to)
        def _():
            pl.semaphore_signal(ready.at[z], inc=1, device_id=on_z(to), device_id_type=MESH)

    def remote(source, target, sent, got, to):
        pltpu.make_async_remote_copy(source, target, sent, got, device_id=to, device_id_type=MESH).start()

    def wait_bytes(ref, sem):
        pltpu.make_async_copy(ref, ref, sem).wait()

    def rows(n):
        return dummy.at[pl.ds(0, n)]

    def send_z(to):
        slots = sl.at[pl.ds(col * 2, 2)]
        remote(s_hbm.at[0, 0, pl.ds(l, 1)], sbuf.at[pl.ds(own, 1)], send.at[0], z_sem.at[z], on_z(to))
        remote(slots, slots, send.at[1], z_sem.at[z], on_z(to))

    def send_x(zs, first):
        block = sbuf.at[pl.ds((l * NZ + zs) * NX + x, 1)]
        slots = sl.at[pl.ds((zs * NX + x) * 2, 2)]
        for step in (2, 1, 3):
            source = s_hbm.at[0, 0, pl.ds(l, 1)] if first else block
            remote(source, block, send.at[0], x_sem.at[zs], on_x(step))
            remote(slots, slots, send.at[1], x_sem.at[zs], on_x(step))

    def send_y(o):
        origin = lax.rem(y - sg * o + NY, NY)
        block = xbuf.at[pl.ds((l * NY + origin) * 2, 2)]
        slots = xl.at[pl.ds(origin * 4, 4)]
        for child, parent in Y_PATH.items():
            if parent == o:
                to = on_y((child - o) % NY)
                got = y_sem.at[Y_ORDER.index(child)]
                source = x_hbm.at[pl.ds(l * 2, 2), 0, 0, 0] if o == 0 else block
                remote(source, block, send.at[3], got, to)
                remote(slots, slots, send.at[4], got, to)

    def share_y(o):
        origin = lax.rem(y - sg * o + NY, NY)
        block = xbuf.at[pl.ds((l * NY + origin) * 2, 2)]
        remote(block, block, send.at[5], sib_x, sibling)

    def group(zs):
        x_tiles, targets, blocks = [], [], []
        for c in range(NX):
            r = (zs % 2) * 4 + c
            m = zs // 2
            xv = xbuf[((m // 2) * NY + r) * 2 + m % 2].reshape(8, 16, B)
            xs = xl[r * 4 + m]
            odd = xs & 1
            put = jnp.broadcast_to(odd.astype(jnp.float32), (16, B)).astype(jnp.bfloat16)[None]
            keep = jnp.broadcast_to((1 - odd).astype(jnp.float32), (16, B)).astype(jnp.bfloat16)[None]
            x_tiles.append(jnp.concatenate([(xv * keep).reshape(B, B), (xv * put).reshape(B, B)], axis=1))
            first_row = l * 8 + (xs >> 1)
            targets.append([sl[(zs * NX + c) * 2 + a] - first_row for a in range(2)])
            blocks.append([sbuf[(a * NZ + zs) * NX + c].reshape(8, 16, B) for a in range(2)])
        x_tile = jnp.concatenate(x_tiles, axis=0)
        for br in range(4):
            row = []
            for c in range(NX):
                hit = [
                    jnp.broadcast_to((targets[c][a] == 2 * br).astype(jnp.float32), (16, B)).astype(jnp.bfloat16)[None]
                    for a in range(2)
                ]
                row.append((blocks[c][0] * hit[0] + blocks[c][1] * hit[1]).reshape(B, B))
            part = jnp.dot(jnp.concatenate(row, axis=1), x_tile, preferred_element_type=jnp.float32)
            if zs == 0:
                out[pl.ds(br * B, B), :] = part
            else:
                out[pl.ds(br * B, B), :] += part

    def product(zs):
        wait_bytes(sbuf.at[pl.ds(0, NX)], sib_s.at[zs])
        group(zs)

    def share_s(zs):
        wait_bytes(rows(198), x_sem.at[zs])
        blocks = sbuf.at[pl.ds((l * NZ + zs) * NX, NX)]
        remote(blocks, blocks, send.at[2], sib_s.at[zs], sibling)

    def send_when_ready(to):
        pl.semaphore_wait(ready.at[to], 1)
        send_z(to)

    def pass_x(zs):
        @pl.when(z != zs)
        def _():
            wait_bytes(rows(66), z_sem.at[zs])
            send_x(zs, False)

    def pass_y(o):
        wait_bytes(rows(132), y_sem.at[Y_ORDER.index(o)])
        send_y(o)
        share_y(o)

    for to in range(NZ - 1):
        @pl.when(z > to)
        def _():
            send_z(to)
    send_x(z, True)
    send_y(0)
    loads[2].wait()
    loads[3].wait()
    share_y(0)
    half = NZ // 2

    @pl.when(z < half)
    def _():
        for zs in range(half):
            @pl.when(z < zs)
            def _():
                send_when_ready(zs)

            pass_x(zs)
        for o in Y_ORDER[:4]:
            pass_y(o)
        for zs in range(half, NZ):
            send_when_ready(zs)
        for zs in range(half, NZ):
            pass_x(zs)

    @pl.when(z >= half)
    def _():
        for zs in range(half + 1, NZ):
            @pl.when(z < zs)
            def _():
                send_when_ready(zs)
        for zs in range(half, NZ):
            pass_x(zs)
        for zs in range(half):
            pass_x(zs)
        for o in Y_ORDER[:4]:
            pass_y(o)

    for o in Y_ORDER[4:]:
        pass_y(o)
    for zs in range(half):
        share_s(zs)
    wait_bytes(xbuf.at[pl.ds(0, 16)], sib_x)
    for zs in range(half):
        product(zs)
    for zs in range(half, NZ):
        share_s(zs)
    for zs in range(half, NZ):
        product(zs)
    wait_bytes(sbuf.at[pl.ds(0, 31)], send.at[0])
    wait_bytes(sl.at[pl.ds(0, 62)], send.at[1])
    wait_bytes(sbuf.at[pl.ds(0, 32)], send.at[2])
    wait_bytes(xbuf.at[pl.ds(0, 14)], send.at[3])
    wait_bytes(xl.at[pl.ds(0, 28)], send.at[4])
    wait_bytes(xbuf.at[pl.ds(0, 16)], send.at[5])


def per_device(s_values, s_slots, x_values, x_slots):
    return pl.pallas_call(
        kernel,
        out_shape=jax.ShapeDtypeStruct((512, 256), jnp.float32),
        in_specs=[pl.BlockSpec(memory_space=pl.ANY)] * 4,
        out_specs=pl.BlockSpec(memory_space=pltpu.VMEM),
        scratch_shapes=[
            pltpu.VMEM((64, B, B), jnp.bfloat16),
            pltpu.VMEM((32, B, B), jnp.bfloat16),
            pltpu.VMEM((64, 1, B), jnp.int32),
            pltpu.VMEM((32, 1, B), jnp.int32),
            pltpu.VMEM((198, 1, B), jnp.int32),
            pltpu.SMEM((1, 1, 2), jnp.int32),
            pltpu.SMEM((1, 1, 1, 4), jnp.int32),
            pltpu.SemaphoreType.DMA((8,)),
            pltpu.SemaphoreType.DMA((8,)),
            pltpu.SemaphoreType.DMA((7,)),
            pltpu.SemaphoreType.DMA((8,)),
            pltpu.SemaphoreType.DMA,
            pltpu.SemaphoreType.DMA((6,)),
            pltpu.SemaphoreType.DMA((4,)),
            pltpu.SemaphoreType.REGULAR((8,)),
        ],
        compiler_params=pltpu.CompilerParams(
            collective_id=0, has_side_effects=True, vmem_limit_bytes=62 * 2**20
        ),
        cost_estimate=pl.CostEstimate(flops=2**30, bytes_accessed=2**20, transcendentals=0),
        name="block_product",
    )(s_values, s_slots, x_values, x_slots.transpose(1, 2, 3, 0))


def solution(mesh):
    placed = (
        P("row", "col", None, None, None),
        P("row", "col", None),
        P(None, "row", "col", None, None, None),
        P(None, "row", "col", None),
    )
    return jax.shard_map(
        per_device,
        mesh=mesh,
        in_specs=placed,
        out_specs=P(("row", "layer"), "col"),
        check_vma=False,
    )
```

```python
import jax
import jax.numpy as jnp
from jax import lax
from jax.experimental import pallas as pl
from jax.experimental.pallas import tpu as pltpu
from jax.sharding import PartitionSpec as P

MESH = pl.DeviceIdType.MESH
NY, NZ, NX = 8, 8, 4
B = 128
Y_PATH = {1: 0, 7: 0, 2: 0, 6: 0, 3: 2, 5: 6, 4: 2}
Y_ORDER = [1, 7, 2, 6, 3, 5, 4]
Y_STEPS = (1, 7, 2, 6)


def kernel(s_hbm, ss_hbm, x_hbm, xs_hbm, out, sbuf, xbuf, sl, xl, dummy, ssm, xsm,
           z_sem, x_sem, y_sem, sib_s, sib_x, send, local, ready):
    y = lax.axis_index("row")
    col = lax.axis_index("col")
    l = lax.axis_index("layer")
    z, x = col // NX, col % NX
    sg = 1 - 2 * l

    def on_z(to):
        return (y, to * NX + x, l)

    def on_x(step):
        return (y, z * NX + lax.rem(x + step, NX), l)

    def on_y(step):
        return (lax.rem(y + sg * step + NY, NY), col, l)

    sibling = (y, col, 1 - l)

    barrier = pltpu.get_barrier_semaphore()
    greeted = [sibling] + [on_x(s) for s in (1, 2, 3)] + [on_y(s) for s in Y_STEPS]
    for peer in greeted:
        pl.semaphore_signal(barrier, inc=1, device_id=peer, device_id_type=MESH)
    for to in range(1, NZ):
        @pl.when(z < to)
        def _():
            pl.semaphore_signal(barrier, inc=1, device_id=on_z(to), device_id_type=MESH)

    own = (l * NZ + z) * NX + x
    loads = [
        pltpu.make_async_copy(ss_hbm, ssm, local.at[0]),
        pltpu.make_async_copy(xs_hbm, xsm, local.at[1]),
        pltpu.make_async_copy(s_hbm.at[0, 0, pl.ds(l, 1)], sbuf.at[pl.ds(own, 1)], local.at[2]),
        pltpu.make_async_copy(
            x_hbm.at[pl.ds(l * 2, 2), 0, 0, 0], xbuf.at[pl.ds((l * NY + y) * 2, 2)], local.at[3]
        ),
    ]
    for load in loads:
        load.start()
    loads[0].wait()
    loads[1].wait()
    for a in range(2):
        sl[col * 2 + a] = jnp.full((1, B), ssm[0, 0, a], jnp.int32)
    for m in range(4):
        xl[y * 4 + m] = jnp.full((1, B), xsm[0, 0, 0, m], jnp.int32)
    pl.semaphore_wait(barrier, len(greeted) + z)
    for to in range(NZ - 1):
        @pl.when(z > to)
        def _():
            pl.semaphore_signal(ready.at[z], inc=1, device_id=on_z(to), device_id_type=MESH)

    def remote(source, target, sent, got, to):
        pltpu.make_async_remote_copy(source, target, sent, got, device_id=to, device_id_type=MESH).start()

    def wait_bytes(ref, sem):
        pltpu.make_async_copy(ref, ref, sem).wait()

    def rows(n):
        return dummy.at[pl.ds(0, n)]

    def send_z(to):
        slots = sl.at[pl.ds(col * 2, 2)]
        remote(s_hbm.at[0, 0, pl.ds(l, 1)], sbuf.at[pl.ds(own, 1)], send.at[0], z_sem.at[z], on_z(to))
        remote(slots, slots, send.at[1], z_sem.at[z], on_z(to))

    def send_x(zs, first):
        block = sbuf.at[pl.ds((l * NZ + zs) * NX + x, 1)]
        slots = sl.at[pl.ds((zs * NX + x) * 2, 2)]
        for step in (2, 1, 3):
            source = s_hbm.at[0, 0, pl.ds(l, 1)] if first else block
            remote(source, block, send.at[0], x_sem.at[zs], on_x(step))
            remote(slots, slots, send.at[1], x_sem.at[zs], on_x(step))

    def send_y(o):
        origin = lax.rem(y - sg * o + NY, NY)
        block = xbuf.at[pl.ds((l * NY + origin) * 2, 2)]
        slots = xl.at[pl.ds(origin * 4, 4)]
        for child, parent in Y_PATH.items():
            if parent == o:
                to = on_y((child - o) % NY)
                got = y_sem.at[Y_ORDER.index(child)]
                source = x_hbm.at[pl.ds(l * 2, 2), 0, 0, 0] if o == 0 else block
                remote(source, block, send.at[3], got, to)
                remote(slots, slots, send.at[4], got, to)

    def share_y(o):
        origin = lax.rem(y - sg * o + NY, NY)
        block = xbuf.at[pl.ds((l * NY + origin) * 2, 2)]
        remote(block, block, send.at[5], sib_x, sibling)

    def group(zs):
        x_tiles, targets, blocks = [], [], []
        for c in range(NX):
            r = (zs % 2) * 4 + c
            m = zs // 2
            xv = xbuf[((m // 2) * NY + r) * 2 + m % 2].reshape(8, 16, B)
            xs = xl[r * 4 + m]
            odd = xs & 1
            put = jnp.broadcast_to(odd.astype(jnp.float32), (16, B)).astype(jnp.bfloat16)[None]
            keep = jnp.broadcast_to((1 - odd).astype(jnp.float32), (16, B)).astype(jnp.bfloat16)[None]
            x_tiles.append(jnp.concatenate([(xv * keep).reshape(B, B), (xv * put).reshape(B, B)], axis=1))
            first_row = l * 8 + (xs >> 1)
            targets.append([sl[(zs * NX + c) * 2 + a] - first_row for a in range(2)])
            blocks.append([sbuf[(a * NZ + zs) * NX + c].reshape(8, 16, B) for a in range(2)])
        x_tile = jnp.concatenate(x_tiles, axis=0)
        for br in range(4):
            row = []
            for c in range(NX):
                hit = [
                    jnp.broadcast_to((targets[c][a] == 2 * br).astype(jnp.float32), (16, B)).astype(jnp.bfloat16)[None]
                    for a in range(2)
                ]
                row.append((blocks[c][0] * hit[0] + blocks[c][1] * hit[1]).reshape(B, B))
            part = jnp.dot(jnp.concatenate(row, axis=1), x_tile, preferred_element_type=jnp.float32)
            if zs == 0:
                out[pl.ds(br * B, B), :] = part
            else:
                out[pl.ds(br * B, B), :] += part

    def product(zs):
        wait_bytes(sbuf.at[pl.ds(0, NX)], sib_s.at[zs])
        group(zs)

    def share_s(zs):
        wait_bytes(rows(198), x_sem.at[zs])
        blocks = sbuf.at[pl.ds((l * NZ + zs) * NX, NX)]
        remote(blocks, blocks, send.at[2], sib_s.at[zs], sibling)

    def send_when_ready(to):
        pl.semaphore_wait(ready.at[to], 1)
        send_z(to)

    def pass_x(zs):
        @pl.when(z != zs)
        def _():
            wait_bytes(rows(66), z_sem.at[zs])
            send_x(zs, False)

    def pass_y(o):
        wait_bytes(rows(132), y_sem.at[Y_ORDER.index(o)])
        send_y(o)
        share_y(o)

    for to in range(NZ - 1):
        @pl.when(z > to)
        def _():
            send_z(to)
    send_x(z, True)
    send_y(0)
    loads[2].wait()
    loads[3].wait()
    share_y(0)
    half = NZ // 2

    @pl.when(z < half)
    def _():
        for zs in range(half):
            @pl.when(z < zs)
            def _():
                send_when_ready(zs)

            pass_x(zs)
        for o in Y_ORDER[:4]:
            pass_y(o)
        for zs in range(half, NZ):
            send_when_ready(zs)
        for zs in range(half, NZ):
            pass_x(zs)
        for o in Y_ORDER[4:]:
            pass_y(o)
        for zs in range(half):
            share_s(zs)

    @pl.when(z >= half)
    def _():
        for zs in range(half + 1, NZ):
            @pl.when(z < zs)
            def _():
                send_when_ready(zs)
        for zs in range(half, NZ):
            pass_x(zs)
        for o in Y_ORDER[:4]:
            pass_y(o)
        for zs in range(half):
            pass_x(zs)
        for o in Y_ORDER[4:]:
            pass_y(o)
        for zs in range(half, NZ):
            share_s(zs)
        for zs in range(half):
            share_s(zs)

    wait_bytes(xbuf.at[pl.ds(0, 16)], sib_x)
    for zs in range(half):
        product(zs)

    @pl.when(z < half)
    def _():
        for zs in range(half, NZ):
            share_s(zs)

    for zs in range(half, NZ):
        product(zs)
    wait_bytes(sbuf.at[pl.ds(0, 31)], send.at[0])
    wait_bytes(sl.at[pl.ds(0, 62)], send.at[1])
    wait_bytes(sbuf.at[pl.ds(0, 32)], send.at[2])
    wait_bytes(xbuf.at[pl.ds(0, 14)], send.at[3])
    wait_bytes(xl.at[pl.ds(0, 28)], send.at[4])
    wait_bytes(xbuf.at[pl.ds(0, 16)], send.at[5])


def per_device(s_values, s_slots, x_values, x_slots):
    return pl.pallas_call(
        kernel,
        out_shape=jax.ShapeDtypeStruct((512, 256), jnp.float32),
        in_specs=[pl.BlockSpec(memory_space=pl.ANY)] * 4,
        out_specs=pl.BlockSpec(memory_space=pltpu.VMEM),
        scratch_shapes=[
            pltpu.VMEM((64, B, B), jnp.bfloat16),
            pltpu.VMEM((32, B, B), jnp.bfloat16),
            pltpu.VMEM((64, 1, B), jnp.int32),
            pltpu.VMEM((32, 1, B), jnp.int32),
            pltpu.VMEM((198, 1, B), jnp.int32),
            pltpu.SMEM((1, 1, 2), jnp.int32),
            pltpu.SMEM((1, 1, 1, 4), jnp.int32),
            pltpu.SemaphoreType.DMA((8,)),
            pltpu.SemaphoreType.DMA((8,)),
            pltpu.SemaphoreType.DMA((7,)),
            pltpu.SemaphoreType.DMA((8,)),
            pltpu.SemaphoreType.DMA,
            pltpu.SemaphoreType.DMA((6,)),
            pltpu.SemaphoreType.DMA((4,)),
            pltpu.SemaphoreType.REGULAR((8,)),
        ],
        compiler_params=pltpu.CompilerParams(
            collective_id=0, has_side_effects=True, vmem_limit_bytes=62 * 2**20
        ),
        cost_estimate=pl.CostEstimate(flops=2**30, bytes_accessed=2**20, transcendentals=0),
        name="block_product",
    )(s_values, s_slots, x_values, x_slots.transpose(1, 2, 3, 0))


def solution(mesh):
    placed = (
        P("row", "col", None, None, None),
        P("row", "col", None),
        P(None, "row", "col", None, None, None),
        P(None, "row", "col", None),
    )
    return jax.shard_map(
        per_device,
        mesh=mesh,
        in_specs=placed,
        out_specs=P(("row", "layer"), "col"),
        check_vma=False,
    )
```

```python
import jax
import jax.numpy as jnp
from jax import lax
from jax.experimental import pallas as pl
from jax.experimental.pallas import tpu as pltpu
from jax.sharding import PartitionSpec as P

MESH = pl.DeviceIdType.MESH
NY, NZ, NX = 8, 8, 4
B = 128
Y_PATH = {1: 0, 7: 0, 2: 0, 6: 0, 3: 2, 5: 6, 4: 2}
Y_ORDER = [1, 7, 2, 6, 3, 5, 4]
Y_STEPS = (1, 7, 2, 6)
LOW = (
    ("y", (1, 7, 2, 6,)),
    ("r", (1,)),
    ("z", (1,)),
    ("r", (2,)),
    ("z", (2,)),
    ("r", (3,)),
    ("z", (3, 0,)),
    ("d", (1, 7, 2, 6,)),
    ("r", (4, 5, 6, 7,)),
    ("z", (4, 5, 6, 7,)),
    ("d", (3, 5, 4,)),
    ("s", (0, 1, 2, 3, 4, 5, 6, 7,)),
)
HIGH = (
    ("y", (1, 7, 2, 6,)),
    ("r", (5, 6, 7,)),
    ("z", (4, 5, 6, 7,)),
    ("d", (1, 7, 2, 6,)),
    ("z", (0, 1, 2, 3,)),
    ("d", (3, 5, 4,)),
    ("s", (4, 5, 6, 7, 0, 1, 2, 3,)),
)


def kernel(s_hbm, ss_hbm, x_hbm, xs_hbm, out, sbuf, xbuf, sl, xl, dummy, ssm, xsm,
           z_sem, x_sem, y_sem, sib_s, sib_x, send, local, ready, y_ready):
    y = lax.axis_index("row")
    col = lax.axis_index("col")
    l = lax.axis_index("layer")
    z, x = col // NX, col % NX
    sg = 1 - 2 * l

    def on_z(to):
        return (y, to * NX + x, l)

    def on_x(step):
        return (y, z * NX + lax.rem(x + step, NX), l)

    def on_y(step):
        return (lax.rem(y + sg * step + NY, NY), col, l)

    sibling = (y, col, 1 - l)

    def rank(at):
        return jnp.where(at < NY // 2, at, NY + 3 - at)

    y_rank = rank(y)
    other = {s: rank(on_y(s)[0]) for s in Y_STEPS}
    barrier = pltpu.get_barrier_semaphore()
    greeted = [sibling] + [on_x(s) for s in (1, 2, 3)]
    for peer in greeted:
        pl.semaphore_signal(barrier, inc=1, device_id=peer, device_id_type=MESH)
    for to in range(1, NZ):
        @pl.when(z < to)
        def _():
            pl.semaphore_signal(barrier, inc=1, device_id=on_z(to), device_id_type=MESH)
    for s in Y_STEPS:
        @pl.when(y_rank < other[s])
        def _():
            pl.semaphore_signal(barrier, inc=1, device_id=on_y(s), device_id_type=MESH)
    expected = len(greeted) + z
    for s in Y_STEPS:
        expected = expected + jnp.where(y_rank > other[s], 1, 0)

    own = (l * NZ + z) * NX + x
    loads = [
        pltpu.make_async_copy(ss_hbm, ssm, local.at[0]),
        pltpu.make_async_copy(xs_hbm, xsm, local.at[1]),
        pltpu.make_async_copy(s_hbm.at[0, 0, pl.ds(l, 1)], sbuf.at[pl.ds(own, 1)], local.at[2]),
        pltpu.make_async_copy(
            x_hbm.at[pl.ds(l * 2, 2), 0, 0, 0], xbuf.at[pl.ds((l * NY + y) * 2, 2)], local.at[3]
        ),
    ]
    for load in loads:
        load.start()
    loads[0].wait()
    loads[1].wait()
    for a in range(2):
        sl[col * 2 + a] = jnp.full((1, B), ssm[0, 0, a], jnp.int32)
    for m in range(4):
        xl[y * 4 + m] = jnp.full((1, B), xsm[0, 0, 0, m], jnp.int32)
    pl.semaphore_wait(barrier, expected)
    for to in range(NZ - 1):
        @pl.when(z > to)
        def _():
            pl.semaphore_signal(ready.at[z], inc=1, device_id=on_z(to), device_id_type=MESH)

    for s in Y_STEPS:
        @pl.when(y_rank > other[s])
        def _():
            pl.semaphore_signal(
                y_ready.at[Y_STEPS.index(-s % NY)], inc=1, device_id=on_y(s), device_id_type=MESH
            )

    def remote(source, target, sent, got, to):
        pltpu.make_async_remote_copy(source, target, sent, got, device_id=to, device_id_type=MESH).start()

    def wait_bytes(ref, sem):
        pltpu.make_async_copy(ref, ref, sem).wait()

    def rows(n):
        return dummy.at[pl.ds(0, n)]

    def send_z(to):
        slots = sl.at[pl.ds(col * 2, 2)]
        remote(s_hbm.at[0, 0, pl.ds(l, 1)], sbuf.at[pl.ds(own, 1)], send.at[0], z_sem.at[z], on_z(to))
        remote(slots, slots, send.at[1], z_sem.at[z], on_z(to))

    def send_x(zs, first):
        block = sbuf.at[pl.ds((l * NZ + zs) * NX + x, 1)]
        slots = sl.at[pl.ds((zs * NX + x) * 2, 2)]
        for step in (2, 1, 3):
            source = s_hbm.at[0, 0, pl.ds(l, 1)] if first else block
            remote(source, block, send.at[0], x_sem.at[zs], on_x(step))
            remote(slots, slots, send.at[1], x_sem.at[zs], on_x(step))

    def send_y(o, only=None):
        origin = lax.rem(y - sg * o + NY, NY)
        block = xbuf.at[pl.ds((l * NY + origin) * 2, 2)]
        slots = xl.at[pl.ds(origin * 4, 4)]
        for child, parent in Y_PATH.items():
            if parent == o and only in (None, child):
                to = on_y((child - o) % NY)
                got = y_sem.at[Y_ORDER.index(child)]
                source = x_hbm.at[pl.ds(l * 2, 2), 0, 0, 0] if o == 0 else block
                remote(source, block, send.at[3], got, to)
                remote(slots, slots, send.at[4], got, to)

    def share_y(o):
        origin = lax.rem(y - sg * o + NY, NY)
        block = xbuf.at[pl.ds((l * NY + origin) * 2, 2)]
        remote(block, block, send.at[5], sib_x, sibling)

    def group(zs):
        x_tiles, targets, blocks = [], [], []
        for c in range(NX):
            r = (zs % 2) * 4 + c
            m = zs // 2
            xv = xbuf[((m // 2) * NY + r) * 2 + m % 2].reshape(8, 16, B)
            xs = xl[r * 4 + m]
            odd = xs & 1
            put = jnp.broadcast_to(odd.astype(jnp.float32), (16, B)).astype(jnp.bfloat16)[None]
            keep = jnp.broadcast_to((1 - odd).astype(jnp.float32), (16, B)).astype(jnp.bfloat16)[None]
            x_tiles.append(jnp.concatenate([(xv * keep).reshape(B, B), (xv * put).reshape(B, B)], axis=1))
            first_row = l * 8 + (xs >> 1)
            targets.append([sl[(zs * NX + c) * 2 + a] - first_row for a in range(2)])
            blocks.append([sbuf[(a * NZ + zs) * NX + c].reshape(8, 16, B) for a in range(2)])
        x_tile = jnp.concatenate(x_tiles, axis=0)
        for br in range(4):
            row = []
            for c in range(NX):
                hit = [
                    jnp.broadcast_to((targets[c][a] == 2 * br).astype(jnp.float32), (16, B)).astype(jnp.bfloat16)[None]
                    for a in range(2)
                ]
                row.append((blocks[c][0] * hit[0] + blocks[c][1] * hit[1]).reshape(B, B))
            part = jnp.dot(jnp.concatenate(row, axis=1), x_tile, preferred_element_type=jnp.float32)
            if zs == 0:
                out[pl.ds(br * B, B), :] = part
            else:
                out[pl.ds(br * B, B), :] += part

    def product(zs):
        wait_bytes(sbuf.at[pl.ds(0, NX)], sib_s.at[zs])
        group(zs)

    def share_s(zs):
        wait_bytes(rows(198), x_sem.at[zs])
        blocks = sbuf.at[pl.ds((l * NZ + zs) * NX, NX)]
        remote(blocks, blocks, send.at[2], sib_s.at[zs], sibling)

    def send_when_ready(to):
        pl.semaphore_wait(ready.at[to], 1)
        send_z(to)

    def pass_x(zs):
        @pl.when(z != zs)
        def _():
            wait_bytes(rows(66), z_sem.at[zs])
            send_x(zs, False)

    def pass_y(o):
        wait_bytes(rows(132), y_sem.at[Y_ORDER.index(o)])
        send_y(o)
        share_y(o)

    def own_y(step):
        @pl.when(y_rank < other[step])
        def _():
            pl.semaphore_wait(y_ready.at[Y_STEPS.index(step)], 1)
        send_y(0, step)

    def run(order):
        for kind, k in [(kind, k) for kind, ks in order for k in ks]:
            if kind == "y":
                own_y(k)
            elif kind == "r":
                @pl.when(z < k)
                def _():
                    send_when_ready(k)
            elif kind == "z":
                pass_x(k)
            elif kind == "d":
                pass_y(k)
            else:
                share_s(k)

    for to in range(NZ - 1):
        @pl.when(z > to)
        def _():
            send_z(to)
    send_x(z, True)
    loads[2].wait()
    loads[3].wait()
    share_y(0)

    @pl.when(z < NZ // 2)
    def _():
        run(LOW)

    @pl.when(z >= NZ // 2)
    def _():
        run(HIGH)

    wait_bytes(xbuf.at[pl.ds(0, 16)], sib_x)
    for zs in range(NZ):
        product(zs)
    wait_bytes(sbuf.at[pl.ds(0, 31)], send.at[0])
    wait_bytes(sl.at[pl.ds(0, 62)], send.at[1])
    wait_bytes(sbuf.at[pl.ds(0, 32)], send.at[2])
    wait_bytes(xbuf.at[pl.ds(0, 14)], send.at[3])
    wait_bytes(xl.at[pl.ds(0, 28)], send.at[4])
    wait_bytes(xbuf.at[pl.ds(0, 16)], send.at[5])


def per_device(s_values, s_slots, x_values, x_slots):
    return pl.pallas_call(
        kernel,
        out_shape=jax.ShapeDtypeStruct((512, 256), jnp.float32),
        in_specs=[pl.BlockSpec(memory_space=pl.ANY)] * 4,
        out_specs=pl.BlockSpec(memory_space=pltpu.VMEM),
        scratch_shapes=[
            pltpu.VMEM((64, B, B), jnp.bfloat16),
            pltpu.VMEM((32, B, B), jnp.bfloat16),
            pltpu.VMEM((64, 1, B), jnp.int32),
            pltpu.VMEM((32, 1, B), jnp.int32),
            pltpu.VMEM((198, 1, B), jnp.int32),
            pltpu.SMEM((1, 1, 2), jnp.int32),
            pltpu.SMEM((1, 1, 1, 4), jnp.int32),
            pltpu.SemaphoreType.DMA((8,)),
            pltpu.SemaphoreType.DMA((8,)),
            pltpu.SemaphoreType.DMA((7,)),
            pltpu.SemaphoreType.DMA((8,)),
            pltpu.SemaphoreType.DMA,
            pltpu.SemaphoreType.DMA((6,)),
            pltpu.SemaphoreType.DMA((4,)),
            pltpu.SemaphoreType.REGULAR((8,)),
            pltpu.SemaphoreType.REGULAR((4,)),
        ],
        compiler_params=pltpu.CompilerParams(
            collective_id=0, has_side_effects=True, vmem_limit_bytes=62 * 2**20
        ),
        cost_estimate=pl.CostEstimate(flops=2**30, bytes_accessed=2**20, transcendentals=0),
        name="block_product",
    )(s_values, s_slots, x_values, x_slots.transpose(1, 2, 3, 0))


def solution(mesh):
    placed = (
        P("row", "col", None, None, None),
        P("row", "col", None),
        P(None, "row", "col", None, None, None),
        P(None, "row", "col", None),
    )
    return jax.shard_map(
        per_device,
        mesh=mesh,
        in_specs=placed,
        out_specs=P(("row", "layer"), "col"),
        check_vma=False,
    )
```

```python
import jax
import jax.numpy as jnp
from jax import lax
from jax.experimental import pallas as pl
from jax.experimental.pallas import tpu as pltpu
from jax.sharding import PartitionSpec as P

MESH = pl.DeviceIdType.MESH
NY, NZ, NX = 8, 8, 4
B = 128
Y_PATH = {1: 0, 7: 0, 2: 0, 6: 0, 3: 2, 5: 6, 4: 2}
Y_ORDER = [1, 7, 2, 6, 3, 5, 4]
Y_STEPS = (1, 7, 2, 6)
LOW = (
    ("y", (1, 7, 2, 6,)),
    ("r", (1,)),
    ("z", (1,)),
    ("r", (2,)),
    ("z", (2,)),
    ("r", (3,)),
    ("z", (3, 0,)),
    ("d", (1, 7, 2, 6,)),
    ("r", (4, 5, 6, 7,)),
    ("z", (4, 5, 6, 7,)),
    ("d", (3, 5, 4,)),
    ("s", (0, 1, 2, 3, 4, 5, 6, 7,)),
)
HIGH = (
    ("y", (1, 7, 2, 6,)),
    ("r", (5, 6, 7,)),
    ("z", (4, 5, 6, 7,)),
    ("d", (1, 7, 2, 6,)),
    ("z", (0, 1, 2, 3,)),
    ("d", (3, 5, 4,)),
    ("s", (4, 5, 6, 7, 0, 1, 2, 3,)),
)


def kernel(s_hbm, ss_hbm, x_hbm, xs_hbm, out, sbuf, xbuf, sl, xl, dummy, ssm, xsm,
           z_sem, x_sem, y_sem, sib_s, sib_x, send, local, ready, y_ready):
    y = lax.axis_index("row")
    col = lax.axis_index("col")
    l = lax.axis_index("layer")
    z, x = col // NX, col % NX
    sg = 1 - 2 * l

    def on_z(to):
        return (y, to * NX + x, l)

    def on_x(step):
        return (y, z * NX + lax.rem(x + step, NX), l)

    def on_y(step):
        return (lax.rem(y + sg * step + NY, NY), col, l)

    sibling = (y, col, 1 - l)

    def rank(at):
        return jnp.where(at < NY // 2, at, NY + 3 - at)

    y_rank = rank(y)
    other = {s: rank(on_y(s)[0]) for s in Y_STEPS}
    barrier = pltpu.get_barrier_semaphore()
    greeted = [sibling] + [on_x(s) for s in (1, 2, 3)]
    for peer in greeted:
        pl.semaphore_signal(barrier, inc=1, device_id=peer, device_id_type=MESH)
    for to in range(1, NZ):
        @pl.when(z < to)
        def _():
            pl.semaphore_signal(barrier, inc=1, device_id=on_z(to), device_id_type=MESH)
    for s in Y_STEPS:
        @pl.when(y_rank < other[s])
        def _():
            pl.semaphore_signal(barrier, inc=1, device_id=on_y(s), device_id_type=MESH)
    expected = len(greeted) + z
    for s in Y_STEPS:
        expected = expected + jnp.where(y_rank > other[s], 1, 0)

    own = (l * NZ + z) * NX + x
    loads = [
        pltpu.make_async_copy(ss_hbm, ssm, local.at[0]),
        pltpu.make_async_copy(xs_hbm, xsm, local.at[1]),
        pltpu.make_async_copy(s_hbm.at[0, 0, pl.ds(l, 1)], sbuf.at[pl.ds(own, 1)], local.at[2]),
        pltpu.make_async_copy(
            x_hbm.at[pl.ds(l * 2, 2), 0, 0, 0], xbuf.at[pl.ds((l * NY + y) * 2, 2)], local.at[3]
        ),
    ]
    for load in loads:
        load.start()
    loads[0].wait()
    loads[1].wait()
    for a in range(2):
        sl[col * 2 + a] = jnp.full((1, B), ssm[0, 0, a], jnp.int32)
    for m in range(4):
        xl[y * 4 + m] = jnp.full((1, B), xsm[0, 0, 0, m], jnp.int32)
    pl.semaphore_wait(barrier, expected)
    for to in range(NZ - 1):
        @pl.when(z > to)
        def _():
            pl.semaphore_signal(ready.at[z], inc=1, device_id=on_z(to), device_id_type=MESH)

    for s in Y_STEPS:
        @pl.when(y_rank > other[s])
        def _():
            pl.semaphore_signal(
                y_ready.at[Y_STEPS.index(-s % NY)], inc=1, device_id=on_y(s), device_id_type=MESH
            )

    def remote(source, target, sent, got, to):
        pltpu.make_async_remote_copy(source, target, sent, got, device_id=to, device_id_type=MESH).start()

    def wait_bytes(ref, sem):
        pltpu.make_async_copy(ref, ref, sem).wait()

    def rows(n):
        return dummy.at[pl.ds(0, n)]

    def send_z(to):
        slots = sl.at[pl.ds(col * 2, 2)]
        remote(s_hbm.at[0, 0, pl.ds(l, 1)], sbuf.at[pl.ds(own, 1)], send.at[0], z_sem.at[z], on_z(to))
        remote(slots, slots, send.at[1], z_sem.at[z], on_z(to))

    def send_x(zs, first):
        block = sbuf.at[pl.ds((l * NZ + zs) * NX + x, 1)]
        slots = sl.at[pl.ds((zs * NX + x) * 2, 2)]
        for step in (2, 1, 3):
            source = s_hbm.at[0, 0, pl.ds(l, 1)] if first else block
            remote(source, block, send.at[0], x_sem.at[zs], on_x(step))
            remote(slots, slots, send.at[1], x_sem.at[zs], on_x(step))

    def send_y(o, only=None):
        origin = lax.rem(y - sg * o + NY, NY)
        block = xbuf.at[pl.ds((l * NY + origin) * 2, 2)]
        slots = xl.at[pl.ds(origin * 4, 4)]
        for child, parent in Y_PATH.items():
            if parent == o and only in (None, child):
                to = on_y((child - o) % NY)
                got = y_sem.at[Y_ORDER.index(child)]
                source = x_hbm.at[pl.ds(l * 2, 2), 0, 0, 0] if o == 0 else block
                remote(source, block, send.at[3], got, to)
                remote(slots, slots, send.at[4], got, to)

    def share_y(o):
        origin = lax.rem(y - sg * o + NY, NY)
        block = xbuf.at[pl.ds((l * NY + origin) * 2, 2)]
        remote(block, block, send.at[5], sib_x, sibling)

    def group(zs):
        x_tiles, targets, blocks = [], [], []
        for c in range(NX):
            r = (zs % 2) * 4 + c
            m = zs // 2
            xv = xbuf[((m // 2) * NY + r) * 2 + m % 2].reshape(8, 16, B)
            xs = xl[r * 4 + m]
            odd = xs & 1
            put = jnp.broadcast_to(odd.astype(jnp.float32), (16, B)).astype(jnp.bfloat16)[None]
            keep = jnp.broadcast_to((1 - odd).astype(jnp.float32), (16, B)).astype(jnp.bfloat16)[None]
            x_tiles.append(jnp.concatenate([(xv * keep).reshape(B, B), (xv * put).reshape(B, B)], axis=1))
            first_row = l * 8 + (xs >> 1)
            targets.append([sl[(zs * NX + c) * 2 + a] - first_row for a in range(2)])
            blocks.append([sbuf[(a * NZ + zs) * NX + c].reshape(8, 16, B) for a in range(2)])
        x_tile = jnp.concatenate(x_tiles, axis=0)
        for br in range(4):
            row = []
            for c in range(NX):
                hit = [
                    jnp.broadcast_to((targets[c][a] == 2 * br).astype(jnp.float32), (16, B)).astype(jnp.bfloat16)[None]
                    for a in range(2)
                ]
                row.append((blocks[c][0] * hit[0] + blocks[c][1] * hit[1]).reshape(B, B))
            part = jnp.dot(jnp.concatenate(row, axis=1), x_tile, preferred_element_type=jnp.float32)
            if zs == 0:
                out[pl.ds(br * B, B), :] = part
            else:
                out[pl.ds(br * B, B), :] += part

    def product(zs):
        wait_bytes(sbuf.at[pl.ds(0, NX)], sib_s.at[zs])
        group(zs)

    def share_s(zs):
        wait_bytes(rows(198), x_sem.at[zs])
        blocks = sbuf.at[pl.ds((l * NZ + zs) * NX, NX)]
        remote(blocks, blocks, send.at[2], sib_s.at[zs], sibling)

    def send_when_ready(to):
        pl.semaphore_wait(ready.at[to], 1)
        send_z(to)

    def pass_x(zs):
        @pl.when(z != zs)
        def _():
            wait_bytes(rows(66), z_sem.at[zs])
            send_x(zs, False)

    def pass_y(o):
        wait_bytes(rows(132), y_sem.at[Y_ORDER.index(o)])
        send_y(o)
        share_y(o)

    def own_y(step):
        @pl.when(y_rank < other[step])
        def _():
            pl.semaphore_wait(y_ready.at[Y_STEPS.index(step)], 1)
        send_y(0, step)

    def run(order):
        for kind, k in [(kind, k) for kind, ks in order for k in ks]:
            if kind == "y":
                own_y(k)
            elif kind == "r":
                @pl.when(z < k)
                def _():
                    send_when_ready(k)
            elif kind == "z":
                pass_x(k)
            elif kind == "d":
                pass_y(k)
            else:
                share_s(k)

    for to in range(NZ - 1):
        @pl.when(z > to)
        def _():
            send_z(to)
    send_x(z, True)
    loads[2].wait()
    loads[3].wait()
    share_y(0)

    @pl.when(z < NZ // 2)
    def _():
        run(LOW)

    @pl.when(z >= NZ // 2)
    def _():
        run(HIGH)

    wait_bytes(xbuf.at[pl.ds(0, 16)], sib_x)
    for zs in range(NZ):
        product(zs)
    wait_bytes(sbuf.at[pl.ds(0, 31)], send.at[0])
    wait_bytes(sl.at[pl.ds(0, 62)], send.at[1])
    wait_bytes(sbuf.at[pl.ds(0, 32)], send.at[2])
    wait_bytes(xbuf.at[pl.ds(0, 14)], send.at[3])
    wait_bytes(xl.at[pl.ds(0, 28)], send.at[4])
    wait_bytes(xbuf.at[pl.ds(0, 16)], send.at[5])


PARTS = 4


def hand_over(made, out, sem):
    rows = out.shape[0] // PARTS
    copies = [
        pltpu.make_async_copy(made.at[pl.ds(i * rows, rows)], out.at[pl.ds(i * rows, rows)], sem.at[i])
        for i in range(PARTS)
    ]
    for copy in copies:
        copy.start()
    for copy in copies:
        copy.wait()


def per_device(s_values, s_slots, x_values, x_slots):
    made = pl.pallas_call(
        kernel,
        out_shape=jax.ShapeDtypeStruct((512, 256), jnp.float32),
        in_specs=[pl.BlockSpec(memory_space=pl.ANY)] * 4,
        out_specs=pl.BlockSpec(memory_space=pltpu.VMEM),
        scratch_shapes=[
            pltpu.VMEM((64, B, B), jnp.bfloat16),
            pltpu.VMEM((32, B, B), jnp.bfloat16),
            pltpu.VMEM((64, 1, B), jnp.int32),
            pltpu.VMEM((32, 1, B), jnp.int32),
            pltpu.VMEM((198, 1, B), jnp.int32),
            pltpu.SMEM((1, 1, 2), jnp.int32),
            pltpu.SMEM((1, 1, 1, 4), jnp.int32),
            pltpu.SemaphoreType.DMA((8,)),
            pltpu.SemaphoreType.DMA((8,)),
            pltpu.SemaphoreType.DMA((7,)),
            pltpu.SemaphoreType.DMA((8,)),
            pltpu.SemaphoreType.DMA,
            pltpu.SemaphoreType.DMA((6,)),
            pltpu.SemaphoreType.DMA((4,)),
            pltpu.SemaphoreType.REGULAR((8,)),
            pltpu.SemaphoreType.REGULAR((4,)),
        ],
        compiler_params=pltpu.CompilerParams(
            collective_id=0, has_side_effects=True, vmem_limit_bytes=62 * 2**20
        ),
        cost_estimate=pl.CostEstimate(flops=2**30, bytes_accessed=2**20, transcendentals=0),
        name="block_product",
    )(s_values, s_slots, x_values, x_slots.transpose(1, 2, 3, 0))
    return pl.pallas_call(
        hand_over,
        out_shape=jax.ShapeDtypeStruct((512, 256), jnp.float32),
        in_specs=[pl.BlockSpec(memory_space=pl.ANY)],
        out_specs=pl.BlockSpec(memory_space=pl.ANY),
        scratch_shapes=[pltpu.SemaphoreType.DMA((PARTS,))],
        compiler_params=pltpu.CompilerParams(vmem_limit_bytes=62 * 2**20),
        name="hand_over",
    )(made)


def solution(mesh):
    placed = (
        P("row", "col", None, None, None),
        P("row", "col", None),
        P(None, "row", "col", None, None, None),
        P(None, "row", "col", None),
    )
    return jax.shard_map(
        per_device,
        mesh=mesh,
        in_specs=placed,
        out_specs=P(("row", "layer"), "col"),
        check_vma=False,
    )
```

```python
import jax
import jax.numpy as jnp
from jax import lax
from jax.experimental import pallas as pl
from jax.experimental.pallas import tpu as pltpu
from jax.sharding import PartitionSpec as P

MESH = pl.DeviceIdType.MESH
NY, NZ, NX = 8, 8, 4
B = 128
Y_PATH = {1: 0, 7: 0, 2: 0, 6: 0, 3: 2, 5: 6, 4: 2}
Y_ORDER = [1, 7, 2, 6, 3, 5, 4]
Y_STEPS = (1, 7, 2, 6)
LOW = (
    ("y", (1, 7, 2, 6,)),
    ("r", (1,)),
    ("z", (1,)),
    ("r", (2,)),
    ("z", (2,)),
    ("r", (3,)),
    ("z", (3, 0,)),
    ("d", (1, 7, 2, 6,)),
    ("r", (4, 5, 6, 7,)),
    ("z", (4, 5, 6, 7,)),
    ("d", (3, 5, 4,)),
    ("s", (0, 1, 2, 3, 4, 5, 6,)),
    ("p", (0, 1, 2, 3, 4,)),
    ("s", (7,)),
    ("p", (5, 6, 7,)),
)
HIGH = (
    ("y", (1, 7, 2, 6,)),
    ("r", (5, 6, 7,)),
    ("z", (4, 5, 6, 7,)),
    ("d", (1, 7, 2, 6,)),
    ("z", (0, 1, 2, 3,)),
    ("d", (3, 5, 4,)),
    ("s", (4, 5, 6, 7, 0, 1, 2,)),
    ("p", (4, 5, 6, 7,)),
    ("s", (3,)),
    ("p", (0, 1, 2, 3,)),
)


def kernel(s_hbm, ss_hbm, x_hbm, xs_hbm, out, sbuf, xbuf, sl, xl, dummy, ssm, xsm,
           z_sem, x_sem, y_sem, sib_s, sib_x, send, local, ready, y_ready):
    y = lax.axis_index("row")
    col = lax.axis_index("col")
    l = lax.axis_index("layer")
    z, x = col // NX, col % NX
    sg = 1 - 2 * l

    def on_z(to):
        return (y, to * NX + x, l)

    def on_x(step):
        return (y, z * NX + lax.rem(x + step, NX), l)

    def on_y(step):
        return (lax.rem(y + sg * step + NY, NY), col, l)

    sibling = (y, col, 1 - l)

    def rank(at):
        return jnp.where(at < NY // 2, at, NY + 3 - at)

    y_rank = rank(y)
    other = {s: rank(on_y(s)[0]) for s in Y_STEPS}
    barrier = pltpu.get_barrier_semaphore()
    greeted = [sibling] + [on_x(s) for s in (1, 2, 3)]
    for peer in greeted:
        pl.semaphore_signal(barrier, inc=1, device_id=peer, device_id_type=MESH)
    for to in range(1, NZ):
        @pl.when(z < to)
        def _():
            pl.semaphore_signal(barrier, inc=1, device_id=on_z(to), device_id_type=MESH)
    for s in Y_STEPS:
        @pl.when(y_rank < other[s])
        def _():
            pl.semaphore_signal(barrier, inc=1, device_id=on_y(s), device_id_type=MESH)
    expected = len(greeted) + z
    for s in Y_STEPS:
        expected = expected + jnp.where(y_rank > other[s], 1, 0)

    own = (l * NZ + z) * NX + x
    loads = [
        pltpu.make_async_copy(ss_hbm, ssm, local.at[0]),
        pltpu.make_async_copy(xs_hbm, xsm, local.at[1]),
        pltpu.make_async_copy(s_hbm.at[0, 0, pl.ds(l, 1)], sbuf.at[pl.ds(own, 1)], local.at[2]),
        pltpu.make_async_copy(
            x_hbm.at[pl.ds(l * 2, 2), 0, 0, 0], xbuf.at[pl.ds((l * NY + y) * 2, 2)], local.at[3]
        ),
    ]
    for load in loads:
        load.start()
    loads[0].wait()
    loads[1].wait()
    for a in range(2):
        sl[col * 2 + a] = jnp.full((1, B), ssm[0, 0, a], jnp.int32)
    for m in range(4):
        xl[y * 4 + m] = jnp.full((1, B), xsm[0, 0, 0, m], jnp.int32)
    pl.semaphore_wait(barrier, expected)
    for to in range(NZ - 1):
        @pl.when(z > to)
        def _():
            pl.semaphore_signal(ready.at[z], inc=1, device_id=on_z(to), device_id_type=MESH)

    for s in Y_STEPS:
        @pl.when(y_rank > other[s])
        def _():
            pl.semaphore_signal(
                y_ready.at[Y_STEPS.index(-s % NY)], inc=1, device_id=on_y(s), device_id_type=MESH
            )

    def remote(source, target, sent, got, to):
        pltpu.make_async_remote_copy(source, target, sent, got, device_id=to, device_id_type=MESH).start()

    def wait_bytes(ref, sem):
        pltpu.make_async_copy(ref, ref, sem).wait()

    def rows(n):
        return dummy.at[pl.ds(0, n)]

    def send_z(to):
        slots = sl.at[pl.ds(col * 2, 2)]
        remote(s_hbm.at[0, 0, pl.ds(l, 1)], sbuf.at[pl.ds(own, 1)], send.at[0], z_sem.at[z], on_z(to))
        remote(slots, slots, send.at[1], z_sem.at[z], on_z(to))

    def send_x(zs, first):
        block = sbuf.at[pl.ds((l * NZ + zs) * NX + x, 1)]
        slots = sl.at[pl.ds((zs * NX + x) * 2, 2)]
        for step in (2, 1, 3):
            source = s_hbm.at[0, 0, pl.ds(l, 1)] if first else block
            remote(source, block, send.at[0], x_sem.at[zs], on_x(step))
            remote(slots, slots, send.at[1], x_sem.at[zs], on_x(step))

    def send_y(o, only=None):
        origin = lax.rem(y - sg * o + NY, NY)
        block = xbuf.at[pl.ds((l * NY + origin) * 2, 2)]
        slots = xl.at[pl.ds(origin * 4, 4)]
        for child, parent in Y_PATH.items():
            if parent == o and only in (None, child):
                to = on_y((child - o) % NY)
                got = y_sem.at[Y_ORDER.index(child)]
                source = x_hbm.at[pl.ds(l * 2, 2), 0, 0, 0] if o == 0 else block
                remote(source, block, send.at[3], got, to)
                remote(slots, slots, send.at[4], got, to)

    def share_y(o):
        origin = lax.rem(y - sg * o + NY, NY)
        block = xbuf.at[pl.ds((l * NY + origin) * 2, 2)]
        remote(block, block, send.at[5], sib_x, sibling)

    def group(zs, first):
        x_tiles, targets, blocks = [], [], []
        for c in range(NX):
            r = (zs % 2) * 4 + c
            m = zs // 2
            xv = xbuf[((m // 2) * NY + r) * 2 + m % 2].reshape(8, 16, B)
            xs = xl[r * 4 + m]
            odd = xs & 1
            put = jnp.broadcast_to(odd.astype(jnp.float32), (16, B)).astype(jnp.bfloat16)[None]
            keep = jnp.broadcast_to((1 - odd).astype(jnp.float32), (16, B)).astype(jnp.bfloat16)[None]
            x_tiles.append(jnp.concatenate([(xv * keep).reshape(B, B), (xv * put).reshape(B, B)], axis=1))
            first_row = l * 8 + (xs >> 1)
            targets.append([sl[(zs * NX + c) * 2 + a] - first_row for a in range(2)])
            blocks.append([sbuf[(a * NZ + zs) * NX + c].reshape(8, 16, B) for a in range(2)])
        x_tile = jnp.concatenate(x_tiles, axis=0)
        for br in range(4):
            row = []
            for c in range(NX):
                hit = [
                    jnp.broadcast_to((targets[c][a] == 2 * br).astype(jnp.float32), (16, B)).astype(jnp.bfloat16)[None]
                    for a in range(2)
                ]
                row.append((blocks[c][0] * hit[0] + blocks[c][1] * hit[1]).reshape(B, B))
            part = jnp.dot(jnp.concatenate(row, axis=1), x_tile, preferred_element_type=jnp.float32)
            if first:
                out[pl.ds(br * B, B), :] = part
            else:
                out[pl.ds(br * B, B), :] += part

    def product(zs, first):
        if first:
            wait_bytes(xbuf.at[pl.ds(0, 16)], sib_x)
        wait_bytes(sbuf.at[pl.ds(0, NX)], sib_s.at[zs])
        group(zs, first)

    def share_s(zs):
        wait_bytes(rows(198), x_sem.at[zs])
        blocks = sbuf.at[pl.ds((l * NZ + zs) * NX, NX)]
        remote(blocks, blocks, send.at[2], sib_s.at[zs], sibling)

    def send_when_ready(to):
        pl.semaphore_wait(ready.at[to], 1)
        send_z(to)

    def pass_x(zs):
        @pl.when(z != zs)
        def _():
            wait_bytes(rows(66), z_sem.at[zs])
            send_x(zs, False)

    def pass_y(o):
        wait_bytes(rows(132), y_sem.at[Y_ORDER.index(o)])
        send_y(o)
        share_y(o)

    def own_y(step):
        @pl.when(y_rank < other[step])
        def _():
            pl.semaphore_wait(y_ready.at[Y_STEPS.index(step)], 1)
        send_y(0, step)

    def run(order, first):
        for kind, k in [(kind, k) for kind, ks in order for k in ks]:
            if kind == "y":
                own_y(k)
            elif kind == "r":
                @pl.when(z < k)
                def _():
                    send_when_ready(k)
            elif kind == "z":
                pass_x(k)
            elif kind == "d":
                pass_y(k)
            elif kind == "p":
                product(k, k == first)
            else:
                share_s(k)

    for to in range(NZ - 1):
        @pl.when(z > to)
        def _():
            send_z(to)
    send_x(z, True)
    loads[2].wait()
    loads[3].wait()
    share_y(0)

    @pl.when(z < NZ // 2)
    def _():
        run(LOW, 0)

    @pl.when(z >= NZ // 2)
    def _():
        run(HIGH, 4)

    wait_bytes(sbuf.at[pl.ds(0, 31)], send.at[0])
    wait_bytes(sl.at[pl.ds(0, 62)], send.at[1])
    wait_bytes(sbuf.at[pl.ds(0, 32)], send.at[2])
    wait_bytes(xbuf.at[pl.ds(0, 14)], send.at[3])
    wait_bytes(xl.at[pl.ds(0, 28)], send.at[4])
    wait_bytes(xbuf.at[pl.ds(0, 16)], send.at[5])


def per_device(s_values, s_slots, x_values, x_slots):
    return pl.pallas_call(
        kernel,
        out_shape=jax.ShapeDtypeStruct((512, 256), jnp.float32),
        in_specs=[pl.BlockSpec(memory_space=pl.ANY)] * 4,
        out_specs=pl.BlockSpec(memory_space=pltpu.VMEM),
        scratch_shapes=[
            pltpu.VMEM((64, B, B), jnp.bfloat16),
            pltpu.VMEM((32, B, B), jnp.bfloat16),
            pltpu.VMEM((64, 1, B), jnp.int32),
            pltpu.VMEM((32, 1, B), jnp.int32),
            pltpu.VMEM((198, 1, B), jnp.int32),
            pltpu.SMEM((1, 1, 2), jnp.int32),
            pltpu.SMEM((1, 1, 1, 4), jnp.int32),
            pltpu.SemaphoreType.DMA((8,)),
            pltpu.SemaphoreType.DMA((8,)),
            pltpu.SemaphoreType.DMA((7,)),
            pltpu.SemaphoreType.DMA((8,)),
            pltpu.SemaphoreType.DMA,
            pltpu.SemaphoreType.DMA((6,)),
            pltpu.SemaphoreType.DMA((4,)),
            pltpu.SemaphoreType.REGULAR((8,)),
            pltpu.SemaphoreType.REGULAR((4,)),
        ],
        compiler_params=pltpu.CompilerParams(
            collective_id=0, has_side_effects=True, vmem_limit_bytes=62 * 2**20
        ),
        cost_estimate=pl.CostEstimate(flops=2**30, bytes_accessed=2**20, transcendentals=0),
        name="block_product",
    )(s_values, s_slots, x_values, x_slots.transpose(1, 2, 3, 0))


def solution(mesh):
    placed = (
        P("row", "col", None, None, None),
        P("row", "col", None),
        P(None, "row", "col", None, None, None),
        P(None, "row", "col", None),
    )
    return jax.shard_map(
        per_device,
        mesh=mesh,
        in_specs=placed,
        out_specs=P(("row", "layer"), "col"),
        check_vma=False,
    )
```

```python
import jax
import jax.numpy as jnp
from jax import lax
from jax.experimental import pallas as pl
from jax.experimental.pallas import tpu as pltpu
from jax.sharding import PartitionSpec as P

MESH = pl.DeviceIdType.MESH
NY, NZ, NX = 8, 8, 4
B = 128
Y_PATH = {1: 0, 7: 0, 2: 0, 6: 0, 3: 2, 5: 6, 4: 2}
Y_ORDER = [1, 7, 2, 6, 3, 5, 4]
Y_STEPS = (1, 7, 2, 6)
LOW = (
    ("y", (1, 7, 2, 6,)),
    ("r", (1,)),
    ("z", (1,)),
    ("r", (2,)),
    ("z", (2,)),
    ("r", (3,)),
    ("z", (3, 0,)),
    ("d", (1, 7, 2, 6,)),
    ("r", (4, 5, 6, 7,)),
    ("z", (4, 5, 6, 7,)),
    ("d", (3, 5, 4,)),
    ("s", (0, 1, 2, 3, 4, 5, 6,)),
    ("p", (0, 1, 2, 3, 4,)),
    ("s", (7,)),
    ("p", (5, 6, 7,)),
)
HIGH = (
    ("y", (1, 7, 2, 6,)),
    ("r", (5, 6, 7,)),
    ("z", (4, 5, 6, 7,)),
    ("d", (1, 7, 2, 6,)),
    ("z", (0, 1, 2, 3,)),
    ("d", (3, 5, 4,)),
    ("s", (4, 5, 6, 7, 0, 1, 2,)),
    ("p", (4, 5, 6, 7,)),
    ("s", (3,)),
    ("p", (0, 1, 2, 3,)),
)


def kernel(s_hbm, ss_hbm, x_hbm, xs_hbm, out, total, sbuf, xbuf, sl, xl, dummy, ssm, xsm,
           z_sem, x_sem, y_sem, sib_s, sib_x, send, local, ready, y_ready):
    y = lax.axis_index("row")
    col = lax.axis_index("col")
    l = lax.axis_index("layer")
    z, x = col // NX, col % NX
    sg = 1 - 2 * l

    def on_z(to):
        return (y, to * NX + x, l)

    def on_x(step):
        return (y, z * NX + lax.rem(x + step, NX), l)

    def on_y(step):
        return (lax.rem(y + sg * step + NY, NY), col, l)

    sibling = (y, col, 1 - l)

    def rank(at):
        return jnp.where(at < NY // 2, at, NY + 3 - at)

    y_rank = rank(y)
    other = {s: rank(on_y(s)[0]) for s in Y_STEPS}
    barrier = pltpu.get_barrier_semaphore()
    greeted = [sibling] + [on_x(s) for s in (1, 2, 3)]
    for peer in greeted:
        pl.semaphore_signal(barrier, inc=1, device_id=peer, device_id_type=MESH)
    for to in range(1, NZ):
        @pl.when(z < to)
        def _():
            pl.semaphore_signal(barrier, inc=1, device_id=on_z(to), device_id_type=MESH)
    for s in Y_STEPS:
        @pl.when(y_rank < other[s])
        def _():
            pl.semaphore_signal(barrier, inc=1, device_id=on_y(s), device_id_type=MESH)
    expected = len(greeted) + z
    for s in Y_STEPS:
        expected = expected + jnp.where(y_rank > other[s], 1, 0)

    own = (l * NZ + z) * NX + x
    loads = [
        pltpu.make_async_copy(ss_hbm, ssm, local.at[0]),
        pltpu.make_async_copy(xs_hbm, xsm, local.at[1]),
        pltpu.make_async_copy(s_hbm.at[0, 0, pl.ds(l, 1)], sbuf.at[pl.ds(own, 1)], local.at[2]),
        pltpu.make_async_copy(
            x_hbm.at[pl.ds(l * 2, 2), 0, 0, 0], xbuf.at[pl.ds((l * NY + y) * 2, 2)], local.at[3]
        ),
    ]
    for load in loads:
        load.start()
    loads[0].wait()
    loads[1].wait()
    for a in range(2):
        sl[col * 2 + a] = jnp.full((1, B), ssm[0, 0, a], jnp.int32)
    for m in range(4):
        xl[y * 4 + m] = jnp.full((1, B), xsm[0, 0, 0, m], jnp.int32)
    pl.semaphore_wait(barrier, expected)
    for to in range(NZ - 1):
        @pl.when(z > to)
        def _():
            pl.semaphore_signal(ready.at[z], inc=1, device_id=on_z(to), device_id_type=MESH)

    for s in Y_STEPS:
        @pl.when(y_rank > other[s])
        def _():
            pl.semaphore_signal(
                y_ready.at[Y_STEPS.index(-s % NY)], inc=1, device_id=on_y(s), device_id_type=MESH
            )

    def remote(source, target, sent, got, to):
        pltpu.make_async_remote_copy(source, target, sent, got, device_id=to, device_id_type=MESH).start()

    def wait_bytes(ref, sem):
        pltpu.make_async_copy(ref, ref, sem).wait()

    def rows(n):
        return dummy.at[pl.ds(0, n)]

    def send_z(to):
        slots = sl.at[pl.ds(col * 2, 2)]
        remote(s_hbm.at[0, 0, pl.ds(l, 1)], sbuf.at[pl.ds(own, 1)], send.at[0], z_sem.at[z], on_z(to))
        remote(slots, slots, send.at[1], z_sem.at[z], on_z(to))

    def send_x(zs, first):
        block = sbuf.at[pl.ds((l * NZ + zs) * NX + x, 1)]
        slots = sl.at[pl.ds((zs * NX + x) * 2, 2)]
        for step in (2, 1, 3):
            source = s_hbm.at[0, 0, pl.ds(l, 1)] if first else block
            remote(source, block, send.at[0], x_sem.at[zs], on_x(step))
            remote(slots, slots, send.at[1], x_sem.at[zs], on_x(step))

    def send_y(o, only=None):
        origin = lax.rem(y - sg * o + NY, NY)
        block = xbuf.at[pl.ds((l * NY + origin) * 2, 2)]
        slots = xl.at[pl.ds(origin * 4, 4)]
        for child, parent in Y_PATH.items():
            if parent == o and only in (None, child):
                to = on_y((child - o) % NY)
                got = y_sem.at[Y_ORDER.index(child)]
                source = x_hbm.at[pl.ds(l * 2, 2), 0, 0, 0] if o == 0 else block
                remote(source, block, send.at[3], got, to)
                remote(slots, slots, send.at[4], got, to)

    def share_y(o):
        origin = lax.rem(y - sg * o + NY, NY)
        block = xbuf.at[pl.ds((l * NY + origin) * 2, 2)]
        remote(block, block, send.at[5], sib_x, sibling)

    def group(zs, first, last):
        x_tiles, targets, blocks = [], [], []
        for c in range(NX):
            r = (zs % 2) * 4 + c
            m = zs // 2
            xv = xbuf[((m // 2) * NY + r) * 2 + m % 2].reshape(8, 16, B)
            xs = xl[r * 4 + m]
            odd = xs & 1
            put = jnp.broadcast_to(odd.astype(jnp.float32), (16, B)).astype(jnp.bfloat16)[None]
            keep = jnp.broadcast_to((1 - odd).astype(jnp.float32), (16, B)).astype(jnp.bfloat16)[None]
            x_tiles.append(jnp.concatenate([(xv * keep).reshape(B, B), (xv * put).reshape(B, B)], axis=1))
            first_row = l * 8 + (xs >> 1)
            targets.append([sl[(zs * NX + c) * 2 + a] - first_row for a in range(2)])
            blocks.append([sbuf[(a * NZ + zs) * NX + c].reshape(8, 16, B) for a in range(2)])
        x_tile = jnp.concatenate(x_tiles, axis=0)
        for br in range(4):
            row = []
            for c in range(NX):
                hit = [
                    jnp.broadcast_to((targets[c][a] == 2 * br).astype(jnp.float32), (16, B)).astype(jnp.bfloat16)[None]
                    for a in range(2)
                ]
                row.append((blocks[c][0] * hit[0] + blocks[c][1] * hit[1]).reshape(B, B))
            part = jnp.dot(jnp.concatenate(row, axis=1), x_tile, preferred_element_type=jnp.float32)
            if first:
                total[pl.ds(br * B, B), :] = part
            else:
                total[pl.ds(br * B, B), :] += part
            if last:
                finished(br).start()

    def finished(br):
        block = pl.ds(br * B, B)
        return pltpu.make_async_copy(total.at[block], out.at[block], local.at[4 + br])

    def product(zs, first, last):
        if first:
            wait_bytes(xbuf.at[pl.ds(0, 16)], sib_x)
        wait_bytes(sbuf.at[pl.ds(0, NX)], sib_s.at[zs])
        group(zs, first, last)

    def share_s(zs):
        wait_bytes(rows(198), x_sem.at[zs])
        blocks = sbuf.at[pl.ds((l * NZ + zs) * NX, NX)]
        remote(blocks, blocks, send.at[2], sib_s.at[zs], sibling)

    def send_when_ready(to):
        pl.semaphore_wait(ready.at[to], 1)
        send_z(to)

    def pass_x(zs):
        @pl.when(z != zs)
        def _():
            wait_bytes(rows(66), z_sem.at[zs])
            send_x(zs, False)

    def pass_y(o):
        wait_bytes(rows(132), y_sem.at[Y_ORDER.index(o)])
        send_y(o)
        share_y(o)

    def own_y(step):
        @pl.when(y_rank < other[step])
        def _():
            pl.semaphore_wait(y_ready.at[Y_STEPS.index(step)], 1)
        send_y(0, step)

    def run(order, first, last):
        for kind, k in [(kind, k) for kind, ks in order for k in ks]:
            if kind == "y":
                own_y(k)
            elif kind == "r":
                @pl.when(z < k)
                def _():
                    send_when_ready(k)
            elif kind == "z":
                pass_x(k)
            elif kind == "d":
                pass_y(k)
            elif kind == "p":
                product(k, k == first, k == last)
            else:
                share_s(k)

    for to in range(NZ - 1):
        @pl.when(z > to)
        def _():
            send_z(to)
    send_x(z, True)
    loads[2].wait()
    loads[3].wait()
    share_y(0)

    @pl.when(z < NZ // 2)
    def _():
        run(LOW, 0, 7)

    @pl.when(z >= NZ // 2)
    def _():
        run(HIGH, 4, 3)

    wait_bytes(sbuf.at[pl.ds(0, 31)], send.at[0])
    wait_bytes(sl.at[pl.ds(0, 62)], send.at[1])
    wait_bytes(sbuf.at[pl.ds(0, 32)], send.at[2])
    wait_bytes(xbuf.at[pl.ds(0, 14)], send.at[3])
    wait_bytes(xl.at[pl.ds(0, 28)], send.at[4])
    wait_bytes(xbuf.at[pl.ds(0, 16)], send.at[5])
    for br in range(4):
        finished(br).wait()


def per_device(s_values, s_slots, x_values, x_slots):
    return pl.pallas_call(
        kernel,
        out_shape=jax.ShapeDtypeStruct((512, 256), jnp.float32),
        in_specs=[pl.BlockSpec(memory_space=pl.ANY)] * 4,
        out_specs=pl.BlockSpec(memory_space=pl.ANY),
        scratch_shapes=[
            pltpu.VMEM((512, 256), jnp.float32),
            pltpu.VMEM((64, B, B), jnp.bfloat16),
            pltpu.VMEM((32, B, B), jnp.bfloat16),
            pltpu.VMEM((64, 1, B), jnp.int32),
            pltpu.VMEM((32, 1, B), jnp.int32),
            pltpu.VMEM((198, 1, B), jnp.int32),
            pltpu.SMEM((1, 1, 2), jnp.int32),
            pltpu.SMEM((1, 1, 1, 4), jnp.int32),
            pltpu.SemaphoreType.DMA((8,)),
            pltpu.SemaphoreType.DMA((8,)),
            pltpu.SemaphoreType.DMA((7,)),
            pltpu.SemaphoreType.DMA((8,)),
            pltpu.SemaphoreType.DMA,
            pltpu.SemaphoreType.DMA((6,)),
            pltpu.SemaphoreType.DMA((8,)),
            pltpu.SemaphoreType.REGULAR((8,)),
            pltpu.SemaphoreType.REGULAR((4,)),
        ],
        compiler_params=pltpu.CompilerParams(
            collective_id=0, has_side_effects=True, vmem_limit_bytes=62 * 2**20
        ),
        cost_estimate=pl.CostEstimate(flops=2**30, bytes_accessed=2**20, transcendentals=0),
        name="block_product",
    )(s_values, s_slots, x_values, x_slots.transpose(1, 2, 3, 0))


def solution(mesh):
    placed = (
        P("row", "col", None, None, None),
        P("row", "col", None),
        P(None, "row", "col", None, None, None),
        P(None, "row", "col", None),
    )
    return jax.shard_map(
        per_device,
        mesh=mesh,
        in_specs=placed,
        out_specs=P(("row", "layer"), "col"),
        check_vma=False,
    )
```

```python
import jax
import jax.numpy as jnp
from jax import lax
from jax.experimental import pallas as pl
from jax.experimental.pallas import tpu as pltpu
from jax.sharding import PartitionSpec as P

MESH = pl.DeviceIdType.MESH
NY, NZ, NX = 8, 8, 4
B = 128
Y_PATH = {1: 0, 7: 0, 2: 0, 6: 0, 3: 2, 5: 6, 4: 2}
Y_ORDER = [1, 7, 2, 6, 3, 5, 4]
Y_STEPS = (1, 7, 2, 6)
LOW = (
    ("y", (1, 7, 2, 6,)),
    ("r", (1,)),
    ("z", (1,)),
    ("r", (2,)),
    ("z", (2,)),
    ("r", (3,)),
    ("z", (3, 0,)),
    ("d", (1, 7, 2, 6,)),
    ("r", (4, 5, 6, 7,)),
    ("z", (4, 5, 6, 7,)),
    ("d", (3, 5, 4,)),
    ("s", (0, 1, 2, 3, 4, 5, 6,)),
    ("p", (0, 1, 2, 3, 4, 5,)),
    ("s", (7,)),
    ("p", (6, 7,)),
)
HIGH = (
    ("y", (1, 7, 2, 6,)),
    ("r", (5, 6, 7,)),
    ("z", (4, 5, 6, 7,)),
    ("d", (1, 7, 2, 6,)),
    ("z", (0, 1, 2, 3,)),
    ("d", (3, 5, 4,)),
    ("s", (4, 5, 6, 7, 0, 1, 2,)),
    ("p", (4, 5, 6, 7, 0, 1,)),
    ("s", (3,)),
    ("p", (2, 3,)),
)


def kernel(s_hbm, ss_hbm, x_hbm, xs_hbm, out, sbuf, xbuf, sl, xl, dummy, ssm, xsm,
           z_sem, x_sem, y_sem, sib_s, sib_x, send, local, ready, y_ready):
    y = lax.axis_index("row")
    col = lax.axis_index("col")
    l = lax.axis_index("layer")
    z, x = col // NX, col % NX
    sg = 1 - 2 * l

    def on_z(to):
        return (y, to * NX + x, l)

    def on_x(step):
        return (y, z * NX + lax.rem(x + step, NX), l)

    def on_y(step):
        return (lax.rem(y + sg * step + NY, NY), col, l)

    sibling = (y, col, 1 - l)

    def rank(at):
        return jnp.where(at < NY // 2, at, NY + 3 - at)

    y_rank = rank(y)
    other = {s: rank(on_y(s)[0]) for s in Y_STEPS}
    barrier = pltpu.get_barrier_semaphore()
    greeted = [sibling] + [on_x(s) for s in (1, 2, 3)]
    for peer in greeted:
        pl.semaphore_signal(barrier, inc=1, device_id=peer, device_id_type=MESH)
    for to in range(1, NZ):
        @pl.when(z < to)
        def _():
            pl.semaphore_signal(barrier, inc=1, device_id=on_z(to), device_id_type=MESH)
    for s in Y_STEPS:
        @pl.when(y_rank < other[s])
        def _():
            pl.semaphore_signal(barrier, inc=1, device_id=on_y(s), device_id_type=MESH)
    expected = len(greeted) + z
    for s in Y_STEPS:
        expected = expected + jnp.where(y_rank > other[s], 1, 0)

    own = (l * NZ + z) * NX + x
    loads = [
        pltpu.make_async_copy(ss_hbm, ssm, local.at[0]),
        pltpu.make_async_copy(xs_hbm, xsm, local.at[1]),
        pltpu.make_async_copy(s_hbm.at[0, 0, pl.ds(l, 1)], sbuf.at[pl.ds(own, 1)], local.at[2]),
        pltpu.make_async_copy(
            x_hbm.at[pl.ds(l * 2, 2), 0, 0, 0], xbuf.at[pl.ds((l * NY + y) * 2, 2)], local.at[3]
        ),
    ]
    for load in loads:
        load.start()
    loads[0].wait()
    loads[1].wait()
    for a in range(2):
        sl[col * 2 + a] = jnp.full((1, B), ssm[0, 0, a], jnp.int32)
    for m in range(4):
        xl[y * 4 + m] = jnp.full((1, B), xsm[0, 0, 0, m], jnp.int32)
    pl.semaphore_wait(barrier, expected)
    for to in range(NZ - 1):
        @pl.when(z > to)
        def _():
            pl.semaphore_signal(ready.at[z], inc=1, device_id=on_z(to), device_id_type=MESH)

    for s in Y_STEPS:
        @pl.when(y_rank > other[s])
        def _():
            pl.semaphore_signal(
                y_ready.at[Y_STEPS.index(-s % NY)], inc=1, device_id=on_y(s), device_id_type=MESH
            )

    def remote(source, target, sent, got, to):
        pltpu.make_async_remote_copy(source, target, sent, got, device_id=to, device_id_type=MESH).start()

    def wait_bytes(ref, sem):
        pltpu.make_async_copy(ref, ref, sem).wait()

    def rows(n):
        return dummy.at[pl.ds(0, n)]

    def send_z(to):
        slots = sl.at[pl.ds(col * 2, 2)]
        remote(s_hbm.at[0, 0, pl.ds(l, 1)], sbuf.at[pl.ds(own, 1)], send.at[0], z_sem.at[z], on_z(to))
        remote(slots, slots, send.at[1], z_sem.at[z], on_z(to))

    def send_x(zs, first):
        block = sbuf.at[pl.ds((l * NZ + zs) * NX + x, 1)]
        slots = sl.at[pl.ds((zs * NX + x) * 2, 2)]
        for step in (2, 1, 3):
            source = s_hbm.at[0, 0, pl.ds(l, 1)] if first else block
            remote(source, block, send.at[0], x_sem.at[zs], on_x(step))
            remote(slots, slots, send.at[1], x_sem.at[zs], on_x(step))

    def send_y(o, only=None):
        origin = lax.rem(y - sg * o + NY, NY)
        block = xbuf.at[pl.ds((l * NY + origin) * 2, 2)]
        slots = xl.at[pl.ds(origin * 4, 4)]
        for child, parent in Y_PATH.items():
            if parent == o and only in (None, child):
                to = on_y((child - o) % NY)
                got = y_sem.at[Y_ORDER.index(child)]
                source = x_hbm.at[pl.ds(l * 2, 2), 0, 0, 0] if o == 0 else block
                remote(source, block, send.at[3], got, to)
                remote(slots, slots, send.at[4], got, to)

    def share_y(o):
        origin = lax.rem(y - sg * o + NY, NY)
        block = xbuf.at[pl.ds((l * NY + origin) * 2, 2)]
        remote(block, block, send.at[5], sib_x, sibling)

    def group(zs, first):
        x_tiles, targets, blocks = [], [], []
        for c in range(NX):
            r = (zs % 2) * 4 + c
            m = zs // 2
            xv = xbuf[((m // 2) * NY + r) * 2 + m % 2].reshape(8, 16, B)
            xs = xl[r * 4 + m]
            odd = xs & 1
            put = jnp.broadcast_to(odd.astype(jnp.float32), (16, B)).astype(jnp.bfloat16)[None]
            keep = jnp.broadcast_to((1 - odd).astype(jnp.float32), (16, B)).astype(jnp.bfloat16)[None]
            x_tiles.append(jnp.concatenate([(xv * keep).reshape(B, B), (xv * put).reshape(B, B)], axis=1))
            first_row = l * 8 + (xs >> 1)
            targets.append([sl[(zs * NX + c) * 2 + a] - first_row for a in range(2)])
            blocks.append([sbuf[(a * NZ + zs) * NX + c].reshape(8, 16, B) for a in range(2)])
        x_tile = jnp.concatenate(x_tiles, axis=0)
        for br in range(4):
            row = []
            for c in range(NX):
                hit = [
                    jnp.broadcast_to((targets[c][a] == 2 * br).astype(jnp.float32), (16, B)).astype(jnp.bfloat16)[None]
                    for a in range(2)
                ]
                row.append((blocks[c][0] * hit[0] + blocks[c][1] * hit[1]).reshape(B, B))
            part = jnp.dot(jnp.concatenate(row, axis=1), x_tile, preferred_element_type=jnp.float32)
            if first:
                out[pl.ds(br * B, B), :] = part
            else:
                out[pl.ds(br * B, B), :] += part

    def product(zs, first):
        if first:
            wait_bytes(xbuf.at[pl.ds(0, 16)], sib_x)
        wait_bytes(sbuf.at[pl.ds(0, NX)], sib_s.at[zs])
        group(zs, first)

    def share_s(zs):
        wait_bytes(rows(198), x_sem.at[zs])
        blocks = sbuf.at[pl.ds((l * NZ + zs) * NX, NX)]
        remote(blocks, blocks, send.at[2], sib_s.at[zs], sibling)

    def send_when_ready(to):
        pl.semaphore_wait(ready.at[to], 1)
        send_z(to)

    def pass_x(zs):
        @pl.when(z != zs)
        def _():
            wait_bytes(rows(66), z_sem.at[zs])
            send_x(zs, False)

    def pass_y(o):
        wait_bytes(rows(132), y_sem.at[Y_ORDER.index(o)])
        send_y(o)
        share_y(o)

    def own_y(step):
        @pl.when(y_rank < other[step])
        def _():
            pl.semaphore_wait(y_ready.at[Y_STEPS.index(step)], 1)
        send_y(0, step)

    def run(order, first):
        for kind, k in [(kind, k) for kind, ks in order for k in ks]:
            if kind == "y":
                own_y(k)
            elif kind == "r":
                @pl.when(z < k)
                def _():
                    send_when_ready(k)
            elif kind == "z":
                pass_x(k)
            elif kind == "d":
                pass_y(k)
            elif kind == "p":
                product(k, k == first)
            else:
                share_s(k)

    for to in range(NZ - 1):
        @pl.when(z > to)
        def _():
            send_z(to)
    send_x(z, True)
    loads[2].wait()
    loads[3].wait()
    share_y(0)

    @pl.when(z < NZ // 2)
    def _():
        run(LOW, 0)

    @pl.when(z >= NZ // 2)
    def _():
        run(HIGH, 4)

    wait_bytes(sbuf.at[pl.ds(0, 31)], send.at[0])
    wait_bytes(sl.at[pl.ds(0, 62)], send.at[1])
    wait_bytes(sbuf.at[pl.ds(0, 32)], send.at[2])
    wait_bytes(xbuf.at[pl.ds(0, 14)], send.at[3])
    wait_bytes(xl.at[pl.ds(0, 28)], send.at[4])
    wait_bytes(xbuf.at[pl.ds(0, 16)], send.at[5])


def per_device(s_values, s_slots, x_values, x_slots):
    return pl.pallas_call(
        kernel,
        out_shape=jax.ShapeDtypeStruct((512, 256), jnp.float32),
        in_specs=[pl.BlockSpec(memory_space=pl.ANY)] * 4,
        out_specs=pl.BlockSpec(memory_space=pltpu.VMEM),
        scratch_shapes=[
            pltpu.VMEM((64, B, B), jnp.bfloat16),
            pltpu.VMEM((32, B, B), jnp.bfloat16),
            pltpu.VMEM((64, 1, B), jnp.int32),
            pltpu.VMEM((32, 1, B), jnp.int32),
            pltpu.VMEM((198, 1, B), jnp.int32),
            pltpu.SMEM((1, 1, 2), jnp.int32),
            pltpu.SMEM((1, 1, 1, 4), jnp.int32),
            pltpu.SemaphoreType.DMA((8,)),
            pltpu.SemaphoreType.DMA((8,)),
            pltpu.SemaphoreType.DMA((7,)),
            pltpu.SemaphoreType.DMA((8,)),
            pltpu.SemaphoreType.DMA,
            pltpu.SemaphoreType.DMA((6,)),
            pltpu.SemaphoreType.DMA((4,)),
            pltpu.SemaphoreType.REGULAR((8,)),
            pltpu.SemaphoreType.REGULAR((4,)),
        ],
        compiler_params=pltpu.CompilerParams(
            collective_id=0, has_side_effects=True, vmem_limit_bytes=62 * 2**20
        ),
        cost_estimate=pl.CostEstimate(flops=2**30, bytes_accessed=2**20, transcendentals=0),
        name="block_product",
    )(s_values, s_slots, x_values, x_slots.transpose(1, 2, 3, 0))


def solution(mesh):
    placed = (
        P("row", "col", None, None, None),
        P("row", "col", None),
        P(None, "row", "col", None, None, None),
        P(None, "row", "col", None),
    )
    return jax.shard_map(
        per_device,
        mesh=mesh,
        in_specs=placed,
        out_specs=P(("row", "layer"), "col"),
        check_vma=False,
    )
```
